512 devices in a mesh: dom: 128 (over z, y_hi, x), cls: 4 (over y_lo, core).
Axes of the slice: x: 4, y: 4 (y_hi: 2, y_lo: 2; y = y_hi * 2 + y_lo), z: 16, core: 2. Of those that a mesh axis runs over, the one named last changes fastest.
Arguments:
- particles: float32 [1024, 64, 256], P('dom'), may hold values from -64 to 64
- references: float32 [128, 16384], P('cls', 'dom'), may hold values from -1 to 1
- noise_var: float32 [64], replicated, may hold values from 0.4 to 2.5
Outputs:
- averages: float32 [128, 16384], P('cls', 'dom')
- noise_new: float32 [64], replicated
- evidence: float32 [1024], P('dom')
The draws below stay inside these ranges and needn't reach their ends.
All inputs are finite; a program needn't handle non-finite values.
Results may differ from the reference program's by a relative error of at most 0.0003.
Values sent between devices are 32-bit elements; how exact they have to be, the bound alone decides.
No kernel may reach another device: no remote copies, remote signals or barrier semaphores. Data moves between devices by JAX's collectives and lax.ppermute only.
A program may use at most 64 MiB of HBM per device.

```python
import math
import jax
import jax.numpy as jnp
from jax import lax

R = 64
A = 256
K = 128
PARTICLES = 1024


def shared_signal(key):
    return jax.random.normal(key, (K, R, A), jnp.float32)


def draw_references(key, part):
    signal = shared_signal(key)
    key = jax.random.fold_in(key, 5)
    own_noise = jax.random.normal(key, (K, R, A), jnp.float32)
    mixed = 0.03 * signal + 0.01 * own_noise
    return jnp.clip(mixed, -1.0, 1.0).reshape(K, R * A)


def rotate_rows(picked, shifts):
    angle_index = (jnp.arange(A, dtype=jnp.int32)[None, :] - shifts[:, None]) % A
    return jnp.take_along_axis(picked, angle_index[:, None, :], axis=2)


def draw_particles(key, part):
    signal = shared_signal(key)
    key = jax.random.fold_in(key, 7)
    label_key, shift_key, noise_key, strength_key, level_key = jax.random.split(key, 5)
    labels = jax.random.randint(label_key, (PARTICLES,), 0, K)
    shifts = jax.random.randint(shift_key, (PARTICLES,), 0, A)
    rotated = rotate_rows(signal[labels], shifts)
    partner = rotate_rows(signal[(labels + 1) % K], shifts)
    spread = 0.6 + 1.2 * jnp.arange(PARTICLES, dtype=jnp.float32) / PARTICLES
    noise_field = jax.random.normal(noise_key, (PARTICLES, R, A), jnp.float32)
    strength = jax.random.uniform(strength_key, (PARTICLES,), jnp.float32, 0.0, 0.08)
    mixed = spread[:, None, None] * noise_field + strength[:, None, None] * rotated
    level = jax.random.uniform(level_key, (PARTICLES,), jnp.float32, 200.0, 400.0)
    amplitude = level / (0.03 * 1.15 * R * A)
    second = amplitude * (1.0 - 2.0 / level)
    strong = amplitude[:, None, None] * rotated + second[:, None, None] * partner + 0.2 * noise_field
    aligned = jnp.arange(PARTICLES, dtype=jnp.int32) % 64 == 0
    mixed = jnp.where(aligned[:, None, None], strong, mixed)
    return jnp.clip(mixed, -64.0, 64.0)


def setup_inputs(seed: int = 0) -> dict:
    arg_keys = jax.random.split(jax.random.key(seed), 4)
    return {
        "particles": draw_particles(jax.random.fold_in(arg_keys[3], 71), 0),
        "references": draw_references(jax.random.fold_in(arg_keys[3], 71), 0),
        "noise_var": jnp.clip(jnp.exp(jax.random.uniform(arg_keys[2], (R,), jnp.float32, math.log(0.4), math.log(2.5))), 0.4, 2.5),
    }


def block_scores(particle_group, ref_fourier, ref_power, inv_noise):
    angles = particle_group.shape[-1]
    fourier = jnp.fft.rfft(particle_group, axis=-1)
    cross_power = jnp.einsum("irm,krm->ikm", fourier * inv_noise[None, :, None], jnp.conj(ref_fourier), precision=lax.Precision.HIGHEST)
    correlation = jnp.fft.irfft(cross_power, n=angles, axis=-1)
    half_norm = 0.5 * jnp.sum(ref_power * inv_noise[None, :], axis=1)
    return correlation - half_norm[None, :, None], fourier


def reference(particles, references, noise_var):
    particle_total, shells, angles = particles.shape
    classes = references.shape[0]
    ref_images = references.reshape(classes, shells, angles)
    group_rows = math.gcd(particle_total, 256)
    grouped = particles.reshape(particle_total // group_rows, group_rows, shells, angles)
    inv_noise = 1.0 / noise_var
    ref_fourier = jnp.fft.rfft(ref_images, axis=-1)
    ref_power = jnp.sum(ref_images * ref_images, axis=2)

    def accumulate(running, particle_group):
        sum_real, sum_imag, occupancy, data_shell = running
        scores, fourier = block_scores(particle_group, ref_fourier, ref_power, inv_noise)
        log_total = jax.nn.logsumexp(scores, axis=(1, 2))
        posterior = jnp.exp(scores - log_total[:, None, None])
        weight_fourier = jnp.fft.rfft(posterior, axis=-1)
        product = jnp.einsum("irm,ikm->krm", fourier, jnp.conj(weight_fourier), precision=lax.Precision.HIGHEST)
        return (sum_real + jnp.real(product), sum_imag + jnp.imag(product), occupancy + jnp.sum(posterior, axis=(0, 2)), data_shell + jnp.sum(particle_group * particle_group, axis=(0, 2))), None

    start_state = (jnp.zeros((classes, shells, angles // 2 + 1), jnp.float32), jnp.zeros((classes, shells, angles // 2 + 1), jnp.float32), jnp.zeros((classes,), jnp.float32), jnp.zeros((shells,), jnp.float32))
    final_state, _ = lax.scan(accumulate, start_state, grouped)
    sum_real, sum_imag, counts, data_shell = final_state
    sum_images = jnp.fft.irfft(lax.complex(sum_real, sum_imag), n=angles, axis=-1)
    cross_shell = jnp.sum(ref_images * sum_images, axis=(0, 2))
    count_power = jnp.sum(counts[:, None] * ref_power, axis=0)
    noise_new = (data_shell - 2.0 * cross_shell + count_power) / (particle_total * angles)
    new_images = sum_images / (counts[:, None, None] + 1.0)
    next_fourier = jnp.fft.rfft(new_images, axis=-1)
    next_power = jnp.sum(new_images * new_images, axis=2)
    next_inv = 1.0 / noise_new

    def group_evidence(particle_group):
        scores, _ = block_scores(particle_group, next_fourier, next_power, next_inv)
        return jax.nn.logsumexp(scores, axis=(1, 2))

    log_next = lax.map(group_evidence, grouped).reshape(particle_total)
    evidence = log_next - jnp.log(jnp.float32(classes * angles))
    return new_images.reshape(classes, shells * angles), noise_new, evidence
```

```python
import jax
import jax.numpy as jnp
import numpy as np
from jax import lax
from jax.experimental import pallas as pl
from jax.experimental.pallas import tpu as pltpu
from jax.sharding import Mesh, PartitionSpec as P

GROUP = ("near", "hx", "cls")
FAR = 8
NEAR = 64
SHELLS = 64
ANGLES = 256
HALF = ANGLES // 2
CLASSES = 128
OWN_CLASSES = 32
OWN_PARTICLES = 2
PARTICLES = 1024
LANES = 128


def dot(left, right, contract=((1,), (0,))):
    return lax.dot_general(
        left,
        right,
        (contract, ((), ())),
        precision=lax.Precision.HIGHEST,
        preferred_element_type=jnp.float32,
    )


def angle_tables():
    angle = np.arange(ANGLES)
    slot = np.arange(HALF)
    radians = (slot[:, None] * angle[None, :] % ANGLES) * (2.0 * np.pi / ANGLES)
    sine = -np.sin(radians)
    sine[0] = np.where(angle % 2 == 0, 1.0, -1.0)
    forward = np.concatenate([np.cos(radians), sine], axis=0)
    weight = np.where(slot == 0, 1.0, 2.0) / ANGLES
    inverse = forward * np.concatenate([weight, weight])[:, None]
    return (
        jnp.asarray(forward.astype(np.float32)),
        jnp.asarray(np.ascontiguousarray(inverse.T).astype(np.float32)),
    )


def rows(base, count, stride):
    return pl.ds(base, count, stride=stride)


def halves(image, part):
    return image[:, part * SHELLS : (part + 1) * SHELLS]


SPREAD = 6
MODEL = 33
CROSS = 8
WEIGHT = 9
SUMS = 34
FINAL = 10


def spread_kernel(place, inv_noise, forward, particles, references, out):
    quarter, half, shell = place[0], place[1], place[2]
    images = particles[pl.ds(quarter * OWN_PARTICLES, OWN_PARTICLES)]
    images = images.reshape(OWN_PARTICLES * SHELLS, ANGLES)
    spectrum = dot(forward[...], images, ((1,), (1,)))
    for i in range(OWN_PARTICLES):
        both = jnp.concatenate(
            [halves(spectrum[:HALF], i), halves(spectrum[HALF:], i)], axis=1
        )
        for m in range(2):
            out[rows(i * 2 + m, NEAR, SPREAD), :] = both[m * NEAR : (m + 1) * NEAR]
    own = references[...]
    table = forward[:, pl.ds(pl.multiple_of(half * HALF, HALF), HALF)]
    model = dot(table, own, ((1,), (1,)))
    pieces = []
    for m in range(2):
        for part in range(2):
            start = part * HALF + m * NEAR
            pieces.append(model[start : start + NEAR])
    out[rows(4, NEAR, SPREAD), :] = jnp.concatenate(pieces, axis=1)
    power = dot(jnp.full((8, LANES), 0.5, jnp.float32), own * own, ((1,), (1,)))
    power = jnp.concatenate([power] * 4, axis=1) * inv_noise[shell]
    lane = lax.broadcasted_iota(jnp.int32, power.shape, 1)
    power = jnp.where(lane // OWN_CLASSES == quarter, power, 0.0)
    out[rows(5, NEAR, SPREAD), :] = jnp.broadcast_to(power[:1], (NEAR, LANES))


def model_kernel(spread, out):
    by_class = []
    for c in range(4):
        first = spread[rows(c * SPREAD + 4, 8, 8 * SPREAD), :]
        second = spread[rows((c + 4) * SPREAD + 4, 8, 8 * SPREAD), :]
        by_class.append(first + second)
    power = jnp.sum(spread[rows(5, NEAR, SPREAD), :], axis=0, keepdims=True)
    pieces = []
    for j in range(4):
        span = slice(j * OWN_CLASSES, (j + 1) * OWN_CLASSES)
        pieces.append(jnp.concatenate([part[:, span] for part in by_class], axis=1))
    block = jnp.concatenate(pieces, axis=0)
    for far in range(FAR):
        out[far * MODEL : far * MODEL + 32, :] = block
        out[far * MODEL + 32 : far * MODEL + 33, :] = power


def model_rows(model, stride, j):
    return jnp.concatenate(
        [model[far * stride + j * 8 : far * stride + j * 8 + 8, :] for far in range(FAR)],
        axis=0,
    )


def particle_rows(spread, m):
    return jnp.concatenate(
        [spread[rows(i * 2 + m, NEAR, SPREAD), :] for i in range(OWN_PARTICLES)], axis=0
    )


def cross_rows(left, real, imag, packed):
    top = jnp.concatenate([real, jnp.where(packed, 0.0, -imag)], axis=1)
    bottom = jnp.concatenate(
        [jnp.where(packed, 0.0, imag), jnp.where(packed, imag, real)], axis=1
    )
    return dot(left, jnp.concatenate([top, bottom], axis=0))


def store_cross(out, stride, m, cross):
    for i in range(OWN_PARTICLES):
        for part in range(2):
            value = cross[i * NEAR : (i + 1) * NEAR, part * LANES : (part + 1) * LANES]
            out[rows(i * 4 + m * 2 + part, NEAR, stride), :] = value


def cross_kernel(place, inv_noise, spread, model, out, half_norm):
    leading = place[3] == 0
    scale = inv_noise[...]
    for m in range(2):
        real = model_rows(model, MODEL, 2 * m) * scale
        imag = model_rows(model, MODEL, 2 * m + 1) * scale
        packed = jnp.logical_and(leading, m == 0)
        store_cross(out, CROSS, m, cross_rows(particle_rows(spread, m), real, imag, packed))
    power = jnp.sum(model[rows(32, FAR, MODEL), :], axis=0, keepdims=True)
    half_norm[...] = jnp.broadcast_to(power, (8, LANES))


def group_scores(cross, stride, inverse, half_norm):
    columns = []
    for i in range(OWN_PARTICLES):
        parts = [
            cross[rows(i * 4 + m * 2 + part, NEAR, stride), :]
            for part in range(2)
            for m in range(2)
        ]
        columns.append(jnp.concatenate(parts, axis=0))
    scores = dot(inverse[...], jnp.concatenate(columns, axis=1))
    return [scores[:, i * LANES : (i + 1) * LANES] - half_norm for i in range(OWN_PARTICLES)]


def whole(reduce, value):
    return reduce(reduce(value, axis=0, keepdims=True), axis=1, keepdims=True)


def posterior_kernel(cross, half_norm, forward, inverse, out):
    posterior = []
    counts = jnp.zeros((1, LANES), jnp.float32)
    for scores in group_scores(cross, CROSS, inverse, half_norm[:1]):
        mass = jnp.exp(scores - whole(jnp.max, scores))
        mass = mass / whole(jnp.sum, mass)
        counts = counts + jnp.sum(mass, axis=0, keepdims=True)
        posterior.append(mass)
    spectrum = dot(forward[...], jnp.concatenate(posterior, axis=1))
    for i in range(OWN_PARTICLES):
        for m in range(2):
            for part in range(2):
                start = part * HALF + m * NEAR
                out[rows(i * 4 + m * 2 + part, NEAR, WEIGHT), :] = spectrum[
                    start : start + NEAR, i * LANES : (i + 1) * LANES
                ]
    out[rows(8, NEAR, WEIGHT), :] = jnp.broadcast_to(counts, (NEAR, LANES))


def sums_kernel(place, spread, model, weight, out):
    leading = place[3] == 0
    counts = jnp.sum(weight[rows(8, NEAR, WEIGHT), :], axis=0, keepdims=True)
    residual = jnp.zeros((SHELLS, LANES), jnp.float32)
    for m in range(2):
        packed = jnp.logical_and(leading, m == 0)
        share = jnp.where(packed, 1.0, 2.0) / ANGLES
        left = particle_rows(spread, m)
        sides = []
        for part in range(2):
            sides.append(
                jnp.concatenate(
                    [
                        weight[rows(i * 4 + m * 2 + part, NEAR, WEIGHT), :]
                        for i in range(OWN_PARTICLES)
                    ],
                    axis=0,
                )
            )
        left_t = left.T
        product = dot(left_t, jnp.concatenate(sides, axis=1))
        real_real = product[:SHELLS, :LANES]
        imag_real = product[SHELLS:, :LANES]
        real_imag = product[:SHELLS, LANES:]
        imag_imag = product[SHELLS:, LANES:]
        real = real_real + jnp.where(packed, 0.0, imag_imag)
        imag = jnp.where(packed, imag_imag, imag_real - real_imag)
        energy = jnp.sum(left_t * left_t, axis=1, keepdims=True)
        residual = residual + (energy[:SHELLS] + energy[SHELLS:]) * (share / LANES)
        for part, value in ((0, real), (1, imag)):
            j = 2 * m + part
            ref = model_rows(model, MODEL, j)
            residual = residual + share * ref * (counts * ref - 2.0 * value)
            for far in range(FAR):
                start = far * SUMS + j * 8
                out[start : start + 8, :] = value[far * 8 : far * 8 + 8]
    power = dot(jnp.ones((8, LANES), jnp.float32), residual, ((1,), (1,)))
    power = jnp.concatenate([power, jnp.zeros_like(power)], axis=1)
    for far in range(FAR):
        start = far * SUMS + 32
        out[start : start + 1, :] = counts
        out[start + 1 : start + 2, :] = power[:1]


def average_kernel(sums, averages, spread_averages, residual):
    total = sums[0:SUMS, :]
    for far in range(1, FAR):
        total = total + sums[far * SUMS : (far + 1) * SUMS, :]
    block = total[:32] / (total[32:33] + 1.0)
    averages[...] = block
    for far in range(FAR):
        spread_averages[far * 32 : far * 32 + 32, :] = block
    residual[...] = jnp.broadcast_to(total[33:34], (NEAR, LANES))


def next_kernel(place, spread, averages, model, residual, out, noise_out):
    leading = place[3] == 0
    noise = jnp.sum(residual[...], axis=0, keepdims=True)[:, :SHELLS]
    noise = noise / (PARTICLES * ANGLES)
    noise_out[...] = noise
    row = lax.broadcasted_iota(jnp.int32, (SHELLS, SHELLS), 0)
    column = lax.broadcasted_iota(jnp.int32, (SHELLS, SHELLS), 1)
    scale = 1.0 / jnp.sum(jnp.where(row == column, noise, 0.0), axis=1, keepdims=True)
    half_norm = jnp.zeros((SHELLS, LANES), jnp.float32)
    for m in range(2):
        packed = jnp.logical_and(leading, m == 0)
        share = jnp.where(packed, 0.5, 1.0) / ANGLES
        real = model_rows(model, 32, 2 * m)
        imag = model_rows(model, 32, 2 * m + 1)
        half_norm = half_norm + share * scale * (real * real + imag * imag)
        cross = cross_rows(particle_rows(spread, m), real * scale, imag * scale, packed)
        store_cross(out, FINAL, m, cross)
    half_norm = jnp.sum(half_norm, axis=0, keepdims=True)
    out[rows(8, NEAR, FINAL), :] = jnp.broadcast_to(half_norm, (NEAR, LANES))
    own = [averages[j * 8 : j * 8 + 8, :] for j in range(4)]
    for c in range(4):
        span = slice(c * OWN_CLASSES, (c + 1) * OWN_CLASSES)
        piece = jnp.concatenate([part[:, span] for part in own], axis=1)
        for side in range(2):
            out[rows((side * 4 + c) * FINAL + 9, 8, 8 * FINAL), :] = piece


def evidence_kernel(place, final, inverse, averages, evidence):
    quarter, half = place[0], place[1]
    half_norm = jnp.sum(final[rows(8, NEAR, FINAL), :], axis=0, keepdims=True)
    lane = lax.broadcasted_iota(jnp.int32, (1, LANES), 1)
    found = jnp.zeros((1, LANES), jnp.float32)
    for i, scores in enumerate(group_scores(final, FINAL, inverse, half_norm)):
        peak = whole(jnp.max, scores)
        total = peak + jnp.log(whole(jnp.sum, jnp.exp(scores - peak)))
        total = total - jnp.log(jnp.full((1, 1), CLASSES * ANGLES, jnp.float32))
        found = found + jnp.where(lane == quarter * OWN_PARTICLES + i, total, 0.0)
    evidence[...] = found
    packed = final[rows(9, NEAR, FINAL), :]
    pieces = []
    for part in range(2):
        for m in range(2):
            j = 2 * m + part
            pieces.append(packed[:, j * OWN_CLASSES : (j + 1) * OWN_CLASSES])
    spectrum = jnp.concatenate(pieces, axis=0)
    table = inverse[pl.ds(pl.multiple_of(half * HALF, HALF), HALF), :]
    averages[...] = dot(table, spectrum).T


SMEM = pl.BlockSpec(memory_space=pltpu.SMEM)
VMEM = pl.BlockSpec(memory_space=pltpu.VMEM)


def call(kernel, shapes, *operands, scalars=0):
    outs = [jax.ShapeDtypeStruct(shape, jnp.float32) for shape in shapes]
    result = pl.pallas_call(
        kernel,
        out_shape=outs if len(outs) > 1 else outs[0],
        in_specs=[SMEM] * scalars + [VMEM] * (len(operands) - scalars),
        out_specs=[VMEM] * len(outs) if len(outs) > 1 else VMEM,
        compiler_params=pltpu.CompilerParams(vmem_limit_bytes=32 * 1024 * 1024),
    )(*operands)
    return result


def exchange(value, axes, count):
    sent = value.reshape(count, 1, value.size // count)
    got = lax.all_to_all(sent, axes, 0, 0, tiled=True)
    return got.reshape(value.shape)


def shards(particles, references, noise_var):
    forward, inverse = angle_tables()
    near, hx, cls = (lax.axis_index(name) for name in GROUP)
    far = lax.axis_index("far")
    shell = far * 8 + near * 4 + hx // 2
    leader = near * 32 + hx * 4 + cls
    place = jnp.stack([cls, hx % 2, shell, leader]).astype(jnp.int32)
    inv_noise = 1.0 / noise_var
    with jax.named_scope("spread"):
        spread = call(
            spread_kernel,
            [(NEAR * SPREAD, LANES)],
            place,
            inv_noise,
            forward,
            particles,
            references,
            scalars=2,
        )
        spread = exchange(spread, GROUP, NEAR)
    with jax.named_scope("model"):
        model = call(model_kernel, [(FAR * MODEL, LANES)], spread)
        model = exchange(model, "far", FAR)
    with jax.named_scope("cross"):
        cross, half_norm = call(
            cross_kernel,
            [(NEAR * CROSS, LANES), (8, LANES)],
            place,
            inv_noise.reshape(SHELLS, 1),
            spread,
            model,
            scalars=1,
        )
        cross = exchange(cross, GROUP, NEAR)
    with jax.named_scope("posterior"):
        weight = call(
            posterior_kernel, [(NEAR * WEIGHT, LANES)], cross, half_norm, forward, inverse
        )
        weight = exchange(weight, GROUP, NEAR)
    with jax.named_scope("sums"):
        sums = call(
            sums_kernel, [(FAR * SUMS, LANES)], place, spread, model, weight, scalars=1
        )
        sums = exchange(sums, "far", FAR)
    with jax.named_scope("averages"):
        own, next_model, residual = call(
            average_kernel, [(32, LANES), (FAR * 32, LANES), (NEAR, LANES)], sums
        )
        residual = exchange(residual, GROUP, NEAR)
        next_model = exchange(next_model, "far", FAR)
    with jax.named_scope("next"):
        final, noise_new = call(
            next_kernel,
            [(NEAR * FINAL, LANES), (1, SHELLS)],
            place,
            spread,
            own,
            next_model,
            residual,
            scalars=1,
        )
        final = exchange(final, GROUP, NEAR)
    with jax.named_scope("evidence"):
        averages, evidence = call(
            evidence_kernel,
            [(OWN_CLASSES, LANES), (1, LANES)],
            place,
            final,
            inverse,
            scalars=1,
        )
        evidence = lax.psum(evidence[0, :8], "cls")
    return averages, noise_new.reshape(SHELLS), evidence


def solution(mesh):
    split = Mesh(mesh.devices.reshape(FAR, 2, 8, 4), ("far", "near", "hx", "cls"))
    dom = ("far", "near", "hx")
    return jax.shard_map(
        shards,
        mesh=split,
        in_specs=(P(dom, None, None), P("cls", dom), P()),
        out_specs=(P("cls", dom), P(), P(dom)),
        check_vma=False,
    )
```

```python
import jax
import jax.numpy as jnp
import numpy as np
from jax import lax
from jax.experimental import pallas as pl
from jax.experimental.pallas import tpu as pltpu
from jax.sharding import Mesh, PartitionSpec as P

GROUP = ("near", "h", "x", "cls")
FAR = 8
NEAR = 64
SHELLS = 64
ANGLES = 256
HALF = ANGLES // 2
CLASSES = 128
OWN_CLASSES = 32
OWN_PARTICLES = 2
PARTICLES = 1024
LANES = 128


def dot(left, right, contract=((1,), (0,))):
    return lax.dot_general(
        left,
        right,
        (contract, ((), ())),
        precision=lax.Precision.HIGHEST,
        preferred_element_type=jnp.float32,
    )


def angle_tables():
    angle = np.arange(ANGLES)
    slot = np.arange(HALF)
    radians = (slot[:, None] * angle[None, :] % ANGLES) * (2.0 * np.pi / ANGLES)
    sine = -np.sin(radians)
    sine[0] = np.where(angle % 2 == 0, 1.0, -1.0)
    forward = np.concatenate([np.cos(radians), sine], axis=0)
    weight = np.where(slot == 0, 1.0, 2.0) / ANGLES
    inverse = forward * np.concatenate([weight, weight])[:, None]
    return (
        jnp.asarray(forward.astype(np.float32)),
        jnp.asarray(np.ascontiguousarray(inverse.T).astype(np.float32)),
    )


def place():
    near, h, x, cls = (lax.axis_index(name) for name in GROUP)
    shell = lax.axis_index("far") * 8 + near * 4 + h * 2 + lax.shift_right_logical(x, 1)
    return cls, lax.bitwise_and(x, 1), shell, near * 32 + h * 16 + x * 4 + cls


def rows(base, count, stride):
    return pl.ds(base, count, stride=stride)


def halves(image, part):
    return image[:, part * SHELLS : (part + 1) * SHELLS]


SPREAD = 6
MODEL = 33
CROSS = 8
WEIGHT = 9
SUMS = 33
NEXT = 33
FINAL = 10


def inverse_column(noise):
    row = lax.broadcasted_iota(jnp.int32, (SHELLS, SHELLS), 0)
    column = lax.broadcasted_iota(jnp.int32, (SHELLS, SHELLS), 1)
    return 1.0 / jnp.sum(jnp.where(row == column, noise, 0.0), axis=1, keepdims=True)


def spread_kernel(
    noise_ref, table_ref, particles, references, out, noise, forward, images, own_ref, sems
):
    quarter, half, shell, _ = place()
    first = quarter * OWN_PARTICLES
    copies = [
        pltpu.make_async_copy(noise_ref, noise, sems.at[0]),
        pltpu.make_async_copy(references, own_ref, sems.at[1]),
    ]
    for i in range(OWN_PARTICLES):
        copies.append(
            pltpu.make_async_copy(particles.at[first + i], images.at[i], sems.at[2 + i])
        )
    for i in range(4):
        span = pl.ds(i * NEAR, NEAR)
        copies.append(
            pltpu.make_async_copy(table_ref.at[span], forward.at[span], sems.at[4 + i])
        )
    for copy in copies:
        copy.start()
    for copy in copies:
        copy.wait()
    spectrum = dot(
        forward[...], images[...].reshape(OWN_PARTICLES * SHELLS, ANGLES), ((1,), (1,))
    )
    for i in range(OWN_PARTICLES):
        both = jnp.concatenate(
            [halves(spectrum[:HALF], i), halves(spectrum[HALF:], i)], axis=1
        )
        for m in range(2):
            out[rows(i * 2 + m, NEAR, SPREAD), :] = both[m * NEAR : (m + 1) * NEAR]
    own = own_ref[...]
    table = forward[:, pl.ds(pl.multiple_of(half * HALF, HALF), HALF)]
    model = dot(table, own, ((1,), (1,)))
    pieces = []
    for m in range(2):
        for part in range(2):
            start = part * HALF + m * NEAR
            pieces.append(model[start : start + NEAR])
    out[rows(4, NEAR, SPREAD), :] = jnp.concatenate(pieces, axis=1)
    power = dot(jnp.full((8, LANES), 0.5, jnp.float32), own * own, ((1,), (1,)))
    lane = lax.broadcasted_iota(jnp.int32, (1, SHELLS), 1)
    own_noise = jnp.sum(jnp.where(lane == shell, noise[...], 0.0), axis=1, keepdims=True)
    power = jnp.concatenate([power] * 4, axis=1) * (1.0 / own_noise)
    lane = lax.broadcasted_iota(jnp.int32, power.shape, 1)
    power = jnp.where(lane // OWN_CLASSES == quarter, power, 0.0)
    passed = jnp.concatenate([noise[...], jnp.zeros((1, SHELLS), jnp.float32)], axis=1)
    power = power[:1] + jnp.where(quarter == 3, passed, 0.0)
    out[rows(5, NEAR, SPREAD), :] = jnp.broadcast_to(power, (NEAR, LANES))


def model_kernel(spread, out):
    by_class = []
    for c in range(4):
        first = spread[rows(c * SPREAD + 4, 8, 8 * SPREAD), :]
        second = spread[rows((c + 4) * SPREAD + 4, 8, 8 * SPREAD), :]
        by_class.append(first + second)
    power = spread[rows(5, NEAR, SPREAD), :]
    lane = lax.broadcasted_iota(jnp.int32, power.shape, 1)
    sender = lax.broadcasted_iota(jnp.int32, power.shape, 0)
    own = lax.shift_right_logical(lane, 5) == lax.bitwise_and(sender, 3)
    power = jnp.sum(jnp.where(own, power, 0.0), axis=0, keepdims=True)
    pieces = []
    for j in range(4):
        span = slice(j * OWN_CLASSES, (j + 1) * OWN_CLASSES)
        pieces.append(jnp.concatenate([part[:, span] for part in by_class], axis=1))
    block = jnp.concatenate(pieces, axis=0)
    for far in range(FAR):
        out[far * MODEL : far * MODEL + 32, :] = block
        out[far * MODEL + 32 : far * MODEL + 33, :] = power


def model_rows(model, stride, j):
    return jnp.concatenate(
        [model[far * stride + j * 8 : far * stride + j * 8 + 8, :] for far in range(FAR)],
        axis=0,
    )


def particle_rows(spread, m):
    return jnp.concatenate(
        [spread[rows(i * 2 + m, NEAR, SPREAD), :] for i in range(OWN_PARTICLES)], axis=0
    )


def cross_rows(left, real, imag, packed):
    top = jnp.concatenate([real, jnp.where(packed, 0.0, -imag)], axis=1)
    bottom = jnp.concatenate(
        [jnp.where(packed, 0.0, imag), jnp.where(packed, imag, real)], axis=1
    )
    return dot(left, jnp.concatenate([top, bottom], axis=0))


def store_cross(out, stride, m, cross):
    for i in range(OWN_PARTICLES):
        for part in range(2):
            value = cross[i * NEAR : (i + 1) * NEAR, part * LANES : (part + 1) * LANES]
            out[rows(i * 4 + m * 2 + part, NEAR, stride), :] = value


def cross_kernel(spread, model, out, half_norm):
    leading = place()[3] == 0
    noise = spread[3 * SPREAD + 5 : 3 * SPREAD + 6, :]
    scale = inverse_column(noise[:, :SHELLS])
    for m in range(2):
        real = model_rows(model, MODEL, 2 * m) * scale
        imag = model_rows(model, MODEL, 2 * m + 1) * scale
        packed = jnp.logical_and(leading, m == 0)
        store_cross(out, CROSS, m, cross_rows(particle_rows(spread, m), real, imag, packed))
    power = jnp.sum(model[rows(32, FAR, MODEL), :], axis=0, keepdims=True)
    half_norm[...] = jnp.broadcast_to(power, (8, LANES))


def group_scores(cross, stride, inverse, half_norm):
    columns = []
    for i in range(OWN_PARTICLES):
        parts = [
            cross[rows(i * 4 + m * 2 + part, NEAR, stride), :]
            for part in range(2)
            for m in range(2)
        ]
        columns.append(jnp.concatenate(parts, axis=0))
    scores = dot(inverse[...], jnp.concatenate(columns, axis=1))
    return [scores[:, i * LANES : (i + 1) * LANES] - half_norm for i in range(OWN_PARTICLES)]


def whole(reduce, value):
    return reduce(reduce(value, axis=0, keepdims=True), axis=1, keepdims=True)


def posterior_kernel(cross, half_norm, forward, inverse, out):
    posterior = []
    counts = jnp.zeros((1, LANES), jnp.float32)
    for scores in group_scores(cross, CROSS, inverse, half_norm[:1]):
        mass = jnp.exp(scores - whole(jnp.max, scores))
        mass = mass / whole(jnp.sum, mass)
        counts = counts + jnp.sum(mass, axis=0, keepdims=True)
        posterior.append(mass)
    spectrum = dot(forward[...], jnp.concatenate(posterior, axis=1))
    for i in range(OWN_PARTICLES):
        for m in range(2):
            for part in range(2):
                start = part * HALF + m * NEAR
                out[rows(i * 4 + m * 2 + part, NEAR, WEIGHT), :] = spectrum[
                    start : start + NEAR, i * LANES : (i + 1) * LANES
                ]
    out[rows(8, NEAR, WEIGHT), :] = jnp.broadcast_to(counts, (NEAR, LANES))


def sums_kernel(spread, model, weight, out, power_out):
    leading = place()[3] == 0
    counts = jnp.sum(weight[rows(8, NEAR, WEIGHT), :], axis=0, keepdims=True)
    residual = jnp.zeros((SHELLS, LANES), jnp.float32)
    for m in range(2):
        packed = jnp.logical_and(leading, m == 0)
        share = jnp.where(packed, 1.0, 2.0) / ANGLES
        left = particle_rows(spread, m)
        sides = []
        for part in range(2):
            sides.append(
                jnp.concatenate(
                    [
                        weight[rows(i * 4 + m * 2 + part, NEAR, WEIGHT), :]
                        for i in range(OWN_PARTICLES)
                    ],
                    axis=0,
                )
            )
        left_t = left.T
        product = dot(left_t, jnp.concatenate(sides, axis=1))
        real_real = product[:SHELLS, :LANES]
        imag_real = product[SHELLS:, :LANES]
        real_imag = product[:SHELLS, LANES:]
        imag_imag = product[SHELLS:, LANES:]
        real = real_real + jnp.where(packed, 0.0, imag_imag)
        imag = jnp.where(packed, imag_imag, imag_real - real_imag)
        energy = jnp.sum(left_t * left_t, axis=1, keepdims=True)
        residual = residual + (energy[:SHELLS] + energy[SHELLS:]) * (share / LANES)
        for part, value in ((0, real), (1, imag)):
            j = 2 * m + part
            ref = model_rows(model, MODEL, j)
            residual = residual + share * ref * (counts * ref - 2.0 * value)
            for far in range(FAR):
                start = far * SUMS + j * 8
                out[start : start + 8, :] = value[far * 8 : far * 8 + 8]
    power = dot(jnp.ones((8, LANES), jnp.float32), residual, ((1,), (1,)))
    power = jnp.concatenate([power, jnp.zeros_like(power)], axis=1)
    power_out[...] = jnp.broadcast_to(power[:1], (NEAR, LANES))
    for far in range(FAR):
        start = far * SUMS + 32
        out[start : start + 1, :] = counts


def average_kernel(sums, power, averages, spread_averages):
    total = sums[0:SUMS, :]
    for far in range(1, FAR):
        total = total + sums[far * SUMS : (far + 1) * SUMS, :]
    block = total[:32] / (total[32:33] + 1.0)
    averages[...] = block
    residual = jnp.sum(power[...], axis=0, keepdims=True)
    for far in range(FAR):
        spread_averages[far * NEXT : far * NEXT + 32, :] = block
        spread_averages[far * NEXT + 32 : far * NEXT + 33, :] = residual


def next_kernel(spread, averages, model, out, noise_out):
    leading = place()[3] == 0
    noise = jnp.sum(model[rows(32, FAR, NEXT), :], axis=0, keepdims=True)[:, :SHELLS]
    noise = noise / (PARTICLES * ANGLES)
    noise_out[...] = noise
    scale = inverse_column(noise)
    half_norm = jnp.zeros((SHELLS, LANES), jnp.float32)
    for m in range(2):
        packed = jnp.logical_and(leading, m == 0)
        share = jnp.where(packed, 0.5, 1.0) / ANGLES
        real = model_rows(model, NEXT, 2 * m)
        imag = model_rows(model, NEXT, 2 * m + 1)
        half_norm = half_norm + share * scale * (real * real + imag * imag)
        cross = cross_rows(particle_rows(spread, m), real * scale, imag * scale, packed)
        store_cross(out, FINAL, m, cross)
    half_norm = jnp.sum(half_norm, axis=0, keepdims=True)
    out[rows(8, NEAR, FINAL), :] = jnp.broadcast_to(half_norm, (NEAR, LANES))
    own = [averages[j * 8 : j * 8 + 8, :] for j in range(4)]
    for c in range(4):
        span = slice(c * OWN_CLASSES, (c + 1) * OWN_CLASSES)
        piece = jnp.concatenate([part[:, span] for part in own], axis=1)
        for side in range(2):
            out[rows((side * 4 + c) * FINAL + 9, 8, 8 * FINAL), :] = piece


def evidence_kernel(final, inverse, averages, evidence):
    quarter, half, _, _ = place()
    half_norm = jnp.sum(final[rows(8, NEAR, FINAL), :], axis=0, keepdims=True)
    lane = lax.broadcasted_iota(jnp.int32, (1, LANES), 1)
    found = jnp.zeros((1, LANES), jnp.float32)
    for i, scores in enumerate(group_scores(final, FINAL, inverse, half_norm)):
        peak = whole(jnp.max, scores)
        total = peak + jnp.log(whole(jnp.sum, jnp.exp(scores - peak)))
        total = total - jnp.log(jnp.full((1, 1), CLASSES * ANGLES, jnp.float32))
        found = found + jnp.where(lane == quarter * OWN_PARTICLES + i, total, 0.0)
    evidence[...] = found[:, :8]
    packed = final[rows(9, NEAR, FINAL), :]
    pieces = []
    for part in range(2):
        for m in range(2):
            j = 2 * m + part
            pieces.append(packed[:, j * OWN_CLASSES : (j + 1) * OWN_CLASSES])
    spectrum = jnp.concatenate(pieces, axis=0)
    table = inverse[pl.ds(pl.multiple_of(half * HALF, HALF), HALF), :]
    averages[...] = dot(table, spectrum).T


VMEM = pl.BlockSpec(memory_space=pltpu.VMEM)
HBM = pl.BlockSpec(memory_space=pltpu.HBM)


def call(kernel, shapes, in_specs, *operands, scratch=(), limit=32 * 1024):
    outs = [jax.ShapeDtypeStruct(shape, jnp.float32) for shape in shapes]
    return pl.pallas_call(
        kernel,
        out_shape=outs,
        in_specs=in_specs,
        out_specs=[VMEM] * len(outs),
        scratch_shapes=scratch,
        compiler_params=pltpu.CompilerParams(vmem_limit_bytes=limit * 1024),
    )(*operands)


def exchange(value, axes, count):
    sent = value.reshape(count, 1, value.size // count)
    got = lax.all_to_all(sent, axes, 0, 0, tiled=True)
    return got.reshape(value.shape)


def shards(particles, references, noise_var):
    forward, inverse = angle_tables()
    noise = noise_var.reshape(1, SHELLS)
    with jax.named_scope("spread"):
        (spread,) = call(
            spread_kernel,
            [(NEAR * SPREAD, LANES)],
            [HBM] * 4,
            noise,
            forward,
            particles,
            references,
            scratch=[
                pltpu.VMEM((1, SHELLS), jnp.float32),
                pltpu.VMEM((ANGLES, ANGLES), jnp.float32),
                pltpu.VMEM((OWN_PARTICLES, SHELLS, ANGLES), jnp.float32),
                pltpu.VMEM((OWN_CLASSES, HALF), jnp.float32),
                pltpu.SemaphoreType.DMA((8,)),
            ],
            limit=60 * 1024,
        )
        spread = exchange(spread, GROUP, NEAR)
    with jax.named_scope("model"):
        (model,) = call(model_kernel, [(FAR * MODEL, LANES)], [VMEM], spread)
        model = exchange(model, "far", FAR)
    with jax.named_scope("cross"):
        cross, half_norm = call(
            cross_kernel,
            [(NEAR * CROSS, LANES), (8, LANES)],
            [VMEM] * 2,
            spread,
            model,
        )
        cross = exchange(cross, GROUP, NEAR)
    with jax.named_scope("posterior"):
        (weight,) = call(
            posterior_kernel,
            [(NEAR * WEIGHT, LANES)],
            [VMEM] * 4,
            cross,
            half_norm,
            forward,
            inverse,
        )
        weight = exchange(weight, GROUP, NEAR)
    with jax.named_scope("sums"):
        sums, power = call(
            sums_kernel,
            [(FAR * SUMS, LANES), (NEAR, LANES)],
            [VMEM] * 3,
            spread,
            model,
            weight,
        )
        power = exchange(power, GROUP, NEAR)
        sums, power = lax.optimization_barrier((sums, power))
        sums = exchange(sums, "far", FAR)
    with jax.named_scope("averages"):
        own, next_model = call(
            average_kernel, [(32, LANES), (FAR * NEXT, LANES)], [VMEM] * 2, sums, power
        )
        next_model = exchange(next_model, "far", FAR)
    with jax.named_scope("next"):
        final, noise_new = call(
            next_kernel,
            [(NEAR * FINAL, LANES), (1, SHELLS)],
            [VMEM] * 3,
            spread,
            own,
            next_model,
        )
        final = exchange(final, GROUP, NEAR)
    with jax.named_scope("evidence"):
        averages, evidence = call(
            evidence_kernel,
            [(OWN_CLASSES, LANES), (1, 8)],
            [VMEM] * 2,
            final,
            inverse,
        )
        evidence = lax.psum(evidence.reshape(8), "cls")
    return averages, noise_new.reshape(SHELLS), evidence


def solution(mesh):
    split = Mesh(mesh.devices.reshape(FAR, 2, 2, 4, 4), ("far", "near", "h", "x", "cls"))
    dom = ("far", "near", "h", "x")
    return jax.shard_map(
        shards,
        mesh=split,
        in_specs=(P(dom, None, None), P("cls", dom), P()),
        out_specs=(P("cls", dom), P(), P(dom)),
        check_vma=False,
    )
```

```python
import jax
import jax.numpy as jnp
import numpy as np
from jax import lax
from jax.experimental import pallas as pl
from jax.experimental.pallas import tpu as pltpu
from jax.sharding import Mesh, PartitionSpec as P

GROUP = ("near", "h", "x", "cls")
FAR = 8
NEAR = 64
SHELLS = 64
ANGLES = 256
HALF = ANGLES // 2
CLASSES = 128
OWN_CLASSES = 32
OWN_PARTICLES = 2
PARTICLES = 1024
LANES = 128
FAR_ORDER = [0, 4, 2, 6, 5, 1, 7, 3]
NEAR_ORDER = [
    24, 14, 51, 30, 26, 3, 25, 8, 0, 42, 54, 10, 63, 55, 45, 43,
    7, 52, 12, 38, 58, 48, 1, 28, 31, 15, 40, 60, 41, 4, 53, 36,
    11, 35, 20, 19, 46, 34, 17, 44, 9, 50, 39, 61, 21, 13, 5, 27,
    2, 18, 23, 56, 47, 37, 6, 29, 49, 16, 33, 57, 62, 32, 22, 59,
]
FAR_AT = [FAR_ORDER.index(i) for i in range(FAR)]
NEAR_AT = [NEAR_ORDER.index(i) for i in range(NEAR)]


def dot(left, right, contract=((1,), (0,))):
    return lax.dot_general(
        left,
        right,
        (contract, ((), ())),
        precision=lax.Precision.HIGHEST,
        preferred_element_type=jnp.float32,
    )


def angle_tables():
    angle = np.arange(ANGLES)
    slot = np.arange(HALF)
    radians = (slot[:, None] * angle[None, :] % ANGLES) * (2.0 * np.pi / ANGLES)
    sine = -np.sin(radians)
    sine[0] = np.where(angle % 2 == 0, 1.0, -1.0)
    forward = np.concatenate([np.cos(radians), sine], axis=0)
    weight = np.where(slot == 0, 1.0, 2.0) / ANGLES
    inverse = forward * np.concatenate([weight, weight])[:, None]
    return (
        jnp.asarray(forward.astype(np.float32)),
        jnp.asarray(np.ascontiguousarray(inverse.T).astype(np.float32)),
    )


def place():
    near, h, x, cls = (lax.axis_index(name) for name in GROUP)
    shell = lax.axis_index("far") * 8 + near * 4 + h * 2 + lax.shift_right_logical(x, 1)
    return cls, lax.bitwise_and(x, 1), shell, near * 32 + h * 16 + x * 4 + cls


def rows(base, count, stride):
    return pl.ds(base, count, stride=stride)


def halves(image, part):
    return image[:, part * SHELLS : (part + 1) * SHELLS]


SPREAD = 6
MODEL = 33
CROSS = 8
WEIGHT = 9
SUMS = 33
NEXT = 33
FINAL = 10


def inverse_column(noise):
    row = lax.broadcasted_iota(jnp.int32, (SHELLS, SHELLS), 0)
    column = lax.broadcasted_iota(jnp.int32, (SHELLS, SHELLS), 1)
    return 1.0 / jnp.sum(jnp.where(row == column, noise, 0.0), axis=1, keepdims=True)


def spread_kernel(
    noise_ref, table_ref, particles, references, out, noise, forward, images, own_ref, sems
):
    quarter, half, shell, _ = place()
    first = quarter * OWN_PARTICLES
    copies = [
        pltpu.make_async_copy(noise_ref, noise, sems.at[0]),
        pltpu.make_async_copy(references, own_ref, sems.at[1]),
    ]
    for i in range(OWN_PARTICLES):
        copies.append(
            pltpu.make_async_copy(particles.at[first + i], images.at[i], sems.at[2 + i])
        )
    for i in range(4):
        span = pl.ds(i * NEAR, NEAR)
        copies.append(
            pltpu.make_async_copy(table_ref.at[span], forward.at[span], sems.at[4 + i])
        )
    for copy in copies:
        copy.start()
    for copy in copies:
        copy.wait()
    spectrum = dot(
        forward[...], images[...].reshape(OWN_PARTICLES * SHELLS, ANGLES), ((1,), (1,))
    )
    for i in range(OWN_PARTICLES):
        both = jnp.concatenate(
            [halves(spectrum[:HALF], i), halves(spectrum[HALF:], i)], axis=1
        )
        for m in range(2):
            out[rows(i * 2 + m, NEAR, SPREAD), :] = both[m * NEAR : (m + 1) * NEAR]
    own = own_ref[...]
    table = forward[:, pl.ds(pl.multiple_of(half * HALF, HALF), HALF)]
    model = dot(table, own, ((1,), (1,)))
    pieces = []
    for m in range(2):
        for part in range(2):
            start = part * HALF + m * NEAR
            pieces.append(model[start : start + NEAR])
    out[rows(4, NEAR, SPREAD), :] = jnp.concatenate(pieces, axis=1)
    power = dot(jnp.full((8, LANES), 0.5, jnp.float32), own * own, ((1,), (1,)))
    lane = lax.broadcasted_iota(jnp.int32, (1, SHELLS), 1)
    own_noise = jnp.sum(jnp.where(lane == shell, noise[...], 0.0), axis=1, keepdims=True)
    power = jnp.concatenate([power] * 4, axis=1) * (1.0 / own_noise)
    lane = lax.broadcasted_iota(jnp.int32, power.shape, 1)
    power = jnp.where(lane // OWN_CLASSES == quarter, power, 0.0)
    passed = jnp.concatenate([noise[...], jnp.zeros((1, SHELLS), jnp.float32)], axis=1)
    power = power[:1] + jnp.where(quarter == 3, passed, 0.0)
    out[rows(5, NEAR, SPREAD), :] = jnp.broadcast_to(power, (NEAR, LANES))


def model_kernel(spread, out):
    def sent(shell, side, c, row):
        start = NEAR_AT[shell * 8 + side * 4 + c] * SPREAD + row
        return spread[start : start + 1, :]

    by_class = []
    power = jnp.zeros((1, LANES), jnp.float32)
    lane = lax.broadcasted_iota(jnp.int32, (1, LANES), 1)
    for c in range(4):
        models, powers = [], []
        for side in range(2):
            models.append(
                jnp.concatenate([sent(shell, side, c, 4) for shell in range(8)], axis=0)
            )
            powers.append(
                jnp.concatenate([sent(shell, side, c, 5) for shell in range(8)], axis=0)
            )
        by_class.append(models[0] + models[1])
        total = jnp.sum(powers[0] + powers[1], axis=0, keepdims=True)
        power = power + jnp.where(lane // OWN_CLASSES == c, total, 0.0)
    pieces = []
    for j in range(4):
        span = slice(j * OWN_CLASSES, (j + 1) * OWN_CLASSES)
        pieces.append(jnp.concatenate([part[:, span] for part in by_class], axis=1))
    block = jnp.concatenate(pieces, axis=0)
    for far in range(FAR):
        out[far * MODEL : far * MODEL + 32, :] = block
        out[far * MODEL + 32 : far * MODEL + 33, :] = power


def model_rows(model, stride, j):
    return jnp.concatenate(
        [model[at * stride + j * 8 : at * stride + j * 8 + 8, :] for at in FAR_AT],
        axis=0,
    )


def particle_rows(spread, m):
    return jnp.concatenate(
        [spread[rows(i * 2 + m, NEAR, SPREAD), :] for i in range(OWN_PARTICLES)], axis=0
    )


def cross_rows(left, real, imag, packed):
    top = jnp.concatenate([real, jnp.where(packed, 0.0, -imag)], axis=1)
    bottom = jnp.concatenate(
        [jnp.where(packed, 0.0, imag), jnp.where(packed, imag, real)], axis=1
    )
    return dot(left, jnp.concatenate([top, bottom], axis=0))


def store_cross(out, stride, m, cross):
    for i in range(OWN_PARTICLES):
        for part in range(2):
            value = cross[i * NEAR : (i + 1) * NEAR, part * LANES : (part + 1) * LANES]
            out[rows(i * 4 + m * 2 + part, NEAR, stride), :] = value


def cross_kernel(spread, model, out, half_norm):
    leading = place()[3] == NEAR_ORDER[0]
    start = NEAR_AT[3] * SPREAD + 5
    noise = spread[start : start + 1, :]
    scale = inverse_column(noise[:, :SHELLS])
    for m in range(2):
        real = model_rows(model, MODEL, 2 * m) * scale
        imag = model_rows(model, MODEL, 2 * m + 1) * scale
        packed = jnp.logical_and(leading, m == 0)
        store_cross(out, CROSS, m, cross_rows(particle_rows(spread, m), real, imag, packed))
    power = jnp.sum(model[rows(32, FAR, MODEL), :], axis=0, keepdims=True)
    half_norm[...] = jnp.broadcast_to(power, (8, LANES))


def group_scores(cross, stride, inverse, half_norm):
    columns = []
    for i in range(OWN_PARTICLES):
        parts = [
            cross[rows(i * 4 + m * 2 + part, NEAR, stride), :]
            for part in range(2)
            for m in range(2)
        ]
        columns.append(jnp.concatenate(parts, axis=0))
    scores = dot(inverse[...], jnp.concatenate(columns, axis=1))
    return [scores[:, i * LANES : (i + 1) * LANES] - half_norm for i in range(OWN_PARTICLES)]


def whole(reduce, value):
    return reduce(reduce(value, axis=0, keepdims=True), axis=1, keepdims=True)


def posterior_kernel(cross, half_norm, forward, inverse, out):
    posterior = []
    counts = jnp.zeros((1, LANES), jnp.float32)
    for scores in group_scores(cross, CROSS, inverse, half_norm[:1]):
        mass = jnp.exp(scores - whole(jnp.max, scores))
        mass = mass / whole(jnp.sum, mass)
        counts = counts + jnp.sum(mass, axis=0, keepdims=True)
        posterior.append(mass)
    spectrum = dot(forward[...], jnp.concatenate(posterior, axis=1))
    for i in range(OWN_PARTICLES):
        for m in range(2):
            for part in range(2):
                start = part * HALF + m * NEAR
                out[rows(i * 4 + m * 2 + part, NEAR, WEIGHT), :] = spectrum[
                    start : start + NEAR, i * LANES : (i + 1) * LANES
                ]
    out[rows(8, NEAR, WEIGHT), :] = jnp.broadcast_to(counts, (NEAR, LANES))


def sums_kernel(spread, model, weight, out, power_out):
    leading = place()[3] == NEAR_ORDER[0]
    counts = jnp.sum(weight[rows(8, NEAR, WEIGHT), :], axis=0, keepdims=True)
    residual = jnp.zeros((SHELLS, LANES), jnp.float32)
    for m in range(2):
        packed = jnp.logical_and(leading, m == 0)
        share = jnp.where(packed, 1.0, 2.0) / ANGLES
        left = particle_rows(spread, m)
        sides = []
        for part in range(2):
            sides.append(
                jnp.concatenate(
                    [
                        weight[rows(i * 4 + m * 2 + part, NEAR, WEIGHT), :]
                        for i in range(OWN_PARTICLES)
                    ],
                    axis=0,
                )
            )
        left_t = left.T
        product = dot(left_t, jnp.concatenate(sides, axis=1))
        real_real = product[:SHELLS, :LANES]
        imag_real = product[SHELLS:, :LANES]
        real_imag = product[:SHELLS, LANES:]
        imag_imag = product[SHELLS:, LANES:]
        real = real_real + jnp.where(packed, 0.0, imag_imag)
        imag = jnp.where(packed, imag_imag, imag_real - real_imag)
        energy = jnp.sum(left_t * left_t, axis=1, keepdims=True)
        residual = residual + (energy[:SHELLS] + energy[SHELLS:]) * (share / LANES)
        for part, value in ((0, real), (1, imag)):
            j = 2 * m + part
            ref = model_rows(model, MODEL, j)
            residual = residual + share * ref * (counts * ref - 2.0 * value)
            for far in range(FAR):
                start = FAR_AT[far] * SUMS + j * 8
                out[start : start + 8, :] = value[far * 8 : far * 8 + 8]
    power = dot(jnp.ones((8, LANES), jnp.float32), residual, ((1,), (1,)))
    power = jnp.concatenate([power, jnp.zeros_like(power)], axis=1)
    power_out[...] = jnp.broadcast_to(power[:1], (NEAR, LANES))
    for far in range(FAR):
        start = far * SUMS + 32
        out[start : start + 1, :] = counts


def average_kernel(sums, power, averages, spread_averages):
    total = sums[0:SUMS, :]
    for far in range(1, FAR):
        total = total + sums[far * SUMS : (far + 1) * SUMS, :]
    block = total[:32] / (total[32:33] + 1.0)
    averages[...] = block
    residual = jnp.sum(power[...], axis=0, keepdims=True)
    for far in range(FAR):
        spread_averages[far * NEXT : far * NEXT + 32, :] = block
        spread_averages[far * NEXT + 32 : far * NEXT + 33, :] = residual


def next_kernel(spread, averages, model, out, noise_out):
    leading = place()[3] == NEAR_ORDER[0]
    noise = jnp.sum(model[rows(32, FAR, NEXT), :], axis=0, keepdims=True)[:, :SHELLS]
    noise = noise / (PARTICLES * ANGLES)
    noise_out[...] = noise
    scale = inverse_column(noise)
    half_norm = jnp.zeros((SHELLS, LANES), jnp.float32)
    for m in range(2):
        packed = jnp.logical_and(leading, m == 0)
        share = jnp.where(packed, 0.5, 1.0) / ANGLES
        real = model_rows(model, NEXT, 2 * m)
        imag = model_rows(model, NEXT, 2 * m + 1)
        half_norm = half_norm + share * scale * (real * real + imag * imag)
        cross = cross_rows(particle_rows(spread, m), real * scale, imag * scale, packed)
        store_cross(out, FINAL, m, cross)
    half_norm = jnp.sum(half_norm, axis=0, keepdims=True)
    out[rows(8, NEAR, FINAL), :] = jnp.broadcast_to(half_norm, (NEAR, LANES))
    own = [averages[j * 8 : j * 8 + 8, :] for j in range(4)]
    for c in range(4):
        span = slice(c * OWN_CLASSES, (c + 1) * OWN_CLASSES)
        piece = jnp.concatenate([part[:, span] for part in own], axis=1)
        for side in range(2):
            for shell in range(8):
                start = NEAR_AT[shell * 8 + side * 4 + c] * FINAL + 9
                out[start : start + 1, :] = piece[shell : shell + 1]


def evidence_kernel(final, inverse, averages, evidence):
    quarter, half, _, _ = place()
    half_norm = jnp.sum(final[rows(8, NEAR, FINAL), :], axis=0, keepdims=True)
    lane = lax.broadcasted_iota(jnp.int32, (1, LANES), 1)
    found = jnp.zeros((1, LANES), jnp.float32)
    for i, scores in enumerate(group_scores(final, FINAL, inverse, half_norm)):
        peak = whole(jnp.max, scores)
        total = peak + jnp.log(whole(jnp.sum, jnp.exp(scores - peak)))
        total = total - jnp.log(jnp.full((1, 1), CLASSES * ANGLES, jnp.float32))
        found = found + jnp.where(lane == quarter * OWN_PARTICLES + i, total, 0.0)
    evidence[...] = found[:, :8]
    packed = final[rows(9, NEAR, FINAL), :]
    pieces = []
    for part in range(2):
        for m in range(2):
            j = 2 * m + part
            pieces.append(packed[:, j * OWN_CLASSES : (j + 1) * OWN_CLASSES])
    spectrum = jnp.concatenate(pieces, axis=0)
    table = inverse[pl.ds(pl.multiple_of(half * HALF, HALF), HALF), :]
    averages[...] = dot(table, spectrum).T


VMEM = pl.BlockSpec(memory_space=pltpu.VMEM)
HBM = pl.BlockSpec(memory_space=pltpu.HBM)


def call(kernel, shapes, in_specs, *operands, scratch=(), limit=32 * 1024):
    outs = [jax.ShapeDtypeStruct(shape, jnp.float32) for shape in shapes]
    return pl.pallas_call(
        kernel,
        out_shape=outs,
        in_specs=in_specs,
        out_specs=[VMEM] * len(outs),
        scratch_shapes=scratch,
        compiler_params=pltpu.CompilerParams(vmem_limit_bytes=limit * 1024),
    )(*operands)


def exchange(value, axes, order):
    sent = value.reshape(len(order), 1, value.size // len(order))
    got = lax.all_to_all(sent, axes, 0, 0, tiled=True, axis_index_groups=[order])
    return got.reshape(value.shape)


def shards(particles, references, noise_var):
    forward, inverse = angle_tables()
    noise = noise_var.reshape(1, SHELLS)
    with jax.named_scope("spread"):
        (spread,) = call(
            spread_kernel,
            [(NEAR * SPREAD, LANES)],
            [HBM] * 4,
            noise,
            forward,
            particles,
            references,
            scratch=[
                pltpu.VMEM((1, SHELLS), jnp.float32),
                pltpu.VMEM((ANGLES, ANGLES), jnp.float32),
                pltpu.VMEM((OWN_PARTICLES, SHELLS, ANGLES), jnp.float32),
                pltpu.VMEM((OWN_CLASSES, HALF), jnp.float32),
                pltpu.SemaphoreType.DMA((8,)),
            ],
            limit=60 * 1024,
        )
        spread = exchange(spread, GROUP, NEAR_ORDER)
    with jax.named_scope("model"):
        (model,) = call(model_kernel, [(FAR * MODEL, LANES)], [VMEM], spread)
        model = exchange(model, "far", FAR_ORDER)
    with jax.named_scope("cross"):
        cross, half_norm = call(
            cross_kernel,
            [(NEAR * CROSS, LANES), (8, LANES)],
            [VMEM] * 2,
            spread,
            model,
        )
        cross = exchange(cross, GROUP, NEAR_ORDER)
    with jax.named_scope("posterior"):
        (weight,) = call(
            posterior_kernel,
            [(NEAR * WEIGHT, LANES)],
            [VMEM] * 4,
            cross,
            half_norm,
            forward,
            inverse,
        )
        weight = exchange(weight, GROUP, NEAR_ORDER)
    with jax.named_scope("sums"):
        sums, power = call(
            sums_kernel,
            [(FAR * SUMS, LANES), (NEAR, LANES)],
            [VMEM] * 3,
            spread,
            model,
            weight,
        )
        power = exchange(power, GROUP, NEAR_ORDER)
        sums, power = lax.optimization_barrier((sums, power))
        sums = exchange(sums, "far", FAR_ORDER)
    with jax.named_scope("averages"):
        own, next_model = call(
            average_kernel, [(32, LANES), (FAR * NEXT, LANES)], [VMEM] * 2, sums, power
        )
        next_model = exchange(next_model, "far", FAR_ORDER)
    with jax.named_scope("next"):
        final, noise_new = call(
            next_kernel,
            [(NEAR * FINAL, LANES), (1, SHELLS)],
            [VMEM] * 3,
            spread,
            own,
            next_model,
        )
        final = exchange(final, GROUP, NEAR_ORDER)
    with jax.named_scope("evidence"):
        averages, evidence = call(
            evidence_kernel,
            [(OWN_CLASSES, LANES), (1, 8)],
            [VMEM] * 2,
            final,
            inverse,
        )
        evidence = lax.psum(evidence.reshape(8), "cls")
    return averages, noise_new.reshape(SHELLS), evidence


def solution(mesh):
    split = Mesh(mesh.devices.reshape(FAR, 2, 2, 4, 4), ("far", "near", "h", "x", "cls"))
    dom = ("far", "near", "h", "x")
    return jax.shard_map(
        shards,
        mesh=split,
        in_specs=(P(dom, None, None), P("cls", dom), P()),
        out_specs=(P("cls", dom), P(), P(dom)),
        check_vma=False,
    )
```

```python
import jax
import jax.numpy as jnp
import numpy as np
from jax import lax
from jax.experimental import pallas as pl
from jax.experimental.pallas import tpu as pltpu
from jax.sharding import Mesh, PartitionSpec as P

GROUP = ("near", "h", "x", "cls")
FAR = 8
NEAR = 64
SHELLS = 64
ANGLES = 256
HALF = ANGLES // 2
CLASSES = 128
OWN_CLASSES = 32
OWN_PARTICLES = 2
PARTICLES = 1024
LANES = 128
FAR_ORDER = [0, 4, 2, 6, 5, 1, 7, 3]
NEAR_ORDER = [
    27, 33, 58, 22, 8, 32, 48, 57, 23, 10, 15, 11, 50, 61, 52, 1,
    28, 6, 37, 41, 20, 31, 43, 59, 53, 4, 3, 2, 38, 26, 14, 42,
    63, 17, 45, 44, 60, 47, 55, 12, 16, 5, 35, 25, 21, 19, 34, 24,
    40, 62, 9, 39, 13, 46, 51, 56, 54, 0, 49, 29, 7, 36, 18, 30,
]
FAR_AT = [FAR_ORDER.index(i) for i in range(FAR)]
NEAR_AT = [NEAR_ORDER.index(i) for i in range(NEAR)]


def dot(left, right, contract=((1,), (0,))):
    return lax.dot_general(
        left,
        right,
        (contract, ((), ())),
        precision=lax.Precision.HIGHEST,
        preferred_element_type=jnp.float32,
    )


def angle_tables():
    angle = np.arange(ANGLES)
    slot = np.arange(HALF)
    radians = (slot[:, None] * angle[None, :] % ANGLES) * (2.0 * np.pi / ANGLES)
    sine = -np.sin(radians)
    sine[0] = np.where(angle % 2 == 0, 1.0, -1.0)
    forward = np.concatenate([np.cos(radians), sine], axis=0)
    weight = np.where(slot == 0, 1.0, 2.0) / ANGLES
    inverse = forward * np.concatenate([weight, weight])[:, None]
    return (
        jnp.asarray(forward.astype(np.float32)),
        jnp.asarray(np.ascontiguousarray(inverse.T).astype(np.float32)),
    )


def place():
    near, h, x, cls = (lax.axis_index(name) for name in GROUP)
    shell = lax.axis_index("far") * 8 + near * 4 + h * 2 + lax.shift_right_logical(x, 1)
    return cls, lax.bitwise_and(x, 1), shell, near * 32 + h * 16 + x * 4 + cls


def rows(base, count, stride):
    return pl.ds(base, count, stride=stride)


def halves(image, part):
    return image[:, part * SHELLS : (part + 1) * SHELLS]


SPREAD = 6
MODEL = 33
CROSS = 8
WEIGHT = 9
SUMS = 33
NEXT = 33
FINAL = 10


def inverse_column(noise):
    row = lax.broadcasted_iota(jnp.int32, (SHELLS, SHELLS), 0)
    column = lax.broadcasted_iota(jnp.int32, (SHELLS, SHELLS), 1)
    return 1.0 / jnp.sum(jnp.where(row == column, noise, 0.0), axis=1, keepdims=True)


def spread_kernel(
    noise_ref, table_ref, particles, references, out, noise, forward, images, own_ref, sems
):
    quarter, half, shell, _ = place()
    first = quarter * OWN_PARTICLES
    copies = [
        pltpu.make_async_copy(noise_ref, noise, sems.at[0]),
        pltpu.make_async_copy(references, own_ref, sems.at[1]),
    ]
    for i in range(OWN_PARTICLES):
        copies.append(
            pltpu.make_async_copy(particles.at[first + i], images.at[i], sems.at[2 + i])
        )
    for i in range(4):
        span = pl.ds(i * NEAR, NEAR)
        copies.append(
            pltpu.make_async_copy(table_ref.at[span], forward.at[span], sems.at[4 + i])
        )
    for copy in copies:
        copy.start()
    for copy in copies:
        copy.wait()
    spectrum = dot(
        forward[...], images[...].reshape(OWN_PARTICLES * SHELLS, ANGLES), ((1,), (1,))
    )
    for i in range(OWN_PARTICLES):
        both = jnp.concatenate(
            [halves(spectrum[:HALF], i), halves(spectrum[HALF:], i)], axis=1
        )
        for m in range(2):
            out[rows(i * 2 + m, NEAR, SPREAD), :] = both[m * NEAR : (m + 1) * NEAR]
    own = own_ref[...]
    table = forward[:, pl.ds(pl.multiple_of(half * HALF, HALF), HALF)]
    model = dot(table, own, ((1,), (1,)))
    pieces = []
    for m in range(2):
        for part in range(2):
            start = part * HALF + m * NEAR
            pieces.append(model[start : start + NEAR])
    out[rows(4, NEAR, SPREAD), :] = jnp.concatenate(pieces, axis=1)
    power = dot(jnp.full((8, LANES), 0.5, jnp.float32), own * own, ((1,), (1,)))
    lane = lax.broadcasted_iota(jnp.int32, (1, SHELLS), 1)
    own_noise = jnp.sum(jnp.where(lane == shell, noise[...], 0.0), axis=1, keepdims=True)
    power = jnp.concatenate([power] * 4, axis=1) * (1.0 / own_noise)
    lane = lax.broadcasted_iota(jnp.int32, power.shape, 1)
    power = jnp.where(lane // OWN_CLASSES == quarter, power, 0.0)
    passed = jnp.concatenate([noise[...], jnp.zeros((1, SHELLS), jnp.float32)], axis=1)
    power = power[:1] + jnp.where(quarter == 3, passed, 0.0)
    out[rows(5, NEAR, SPREAD), :] = jnp.broadcast_to(power, (NEAR, LANES))


def model_kernel(spread, out):
    def sent(shell, side, c, row):
        start = NEAR_AT[shell * 8 + side * 4 + c] * SPREAD + row
        return spread[start : start + 1, :]

    by_class = []
    power = jnp.zeros((1, LANES), jnp.float32)
    lane = lax.broadcasted_iota(jnp.int32, (1, LANES), 1)
    for c in range(4):
        models, powers = [], []
        for side in range(2):
            models.append(
                jnp.concatenate([sent(shell, side, c, 4) for shell in range(8)], axis=0)
            )
            powers.append(
                jnp.concatenate([sent(shell, side, c, 5) for shell in range(8)], axis=0)
            )
        by_class.append(models[0] + models[1])
        total = jnp.sum(powers[0] + powers[1], axis=0, keepdims=True)
        power = power + jnp.where(lane // OWN_CLASSES == c, total, 0.0)
    pieces = []
    for j in range(4):
        span = slice(j * OWN_CLASSES, (j + 1) * OWN_CLASSES)
        pieces.append(jnp.concatenate([part[:, span] for part in by_class], axis=1))
    block = jnp.concatenate(pieces, axis=0)
    for far in range(FAR):
        out[far * MODEL : far * MODEL + 32, :] = block
        out[far * MODEL + 32 : far * MODEL + 33, :] = power


def model_rows(model, stride, j):
    return jnp.concatenate(
        [model[at * stride + j * 8 : at * stride + j * 8 + 8, :] for at in FAR_AT],
        axis=0,
    )


def particle_rows(spread, m):
    return jnp.concatenate(
        [spread[rows(i * 2 + m, NEAR, SPREAD), :] for i in range(OWN_PARTICLES)], axis=0
    )


def cross_rows(left, real, imag, packed):
    top = jnp.concatenate([real, jnp.where(packed, 0.0, -imag)], axis=1)
    bottom = jnp.concatenate(
        [jnp.where(packed, 0.0, imag), jnp.where(packed, imag, real)], axis=1
    )
    return dot(left, jnp.concatenate([top, bottom], axis=0))


def store_cross(out, stride, m, cross):
    for i in range(OWN_PARTICLES):
        for part in range(2):
            value = cross[i * NEAR : (i + 1) * NEAR, part * LANES : (part + 1) * LANES]
            out[rows(i * 4 + m * 2 + part, NEAR, stride), :] = value


def cross_kernel(spread, model, out, half_norm):
    leading = place()[3] == NEAR_ORDER[0]
    start = NEAR_AT[3] * SPREAD + 5
    noise = spread[start : start + 1, :]
    scale = inverse_column(noise[:, :SHELLS])
    for m in range(2):
        real = model_rows(model, MODEL, 2 * m) * scale
        imag = model_rows(model, MODEL, 2 * m + 1) * scale
        packed = jnp.logical_and(leading, m == 0)
        store_cross(out, CROSS, m, cross_rows(particle_rows(spread, m), real, imag, packed))
    power = jnp.sum(model[rows(32, FAR, MODEL), :], axis=0, keepdims=True)
    half_norm[...] = jnp.broadcast_to(power, (8, LANES))


def group_scores(cross, stride, inverse, half_norm):
    columns = []
    for i in range(OWN_PARTICLES):
        parts = [
            cross[rows(i * 4 + m * 2 + part, NEAR, stride), :]
            for part in range(2)
            for m in range(2)
        ]
        columns.append(jnp.concatenate(parts, axis=0))
    scores = dot(inverse[...], jnp.concatenate(columns, axis=1))
    return [scores[:, i * LANES : (i + 1) * LANES] - half_norm for i in range(OWN_PARTICLES)]


def whole(reduce, value):
    return reduce(reduce(value, axis=0, keepdims=True), axis=1, keepdims=True)


def posterior_kernel(cross, half_norm, forward, inverse, out):
    posterior = []
    counts = jnp.zeros((1, LANES), jnp.float32)
    for scores in group_scores(cross, CROSS, inverse, half_norm[:1]):
        mass = jnp.exp(scores - whole(jnp.max, scores))
        mass = mass / whole(jnp.sum, mass)
        counts = counts + jnp.sum(mass, axis=0, keepdims=True)
        posterior.append(mass)
    spectrum = dot(forward[...], jnp.concatenate(posterior, axis=1))
    for i in range(OWN_PARTICLES):
        for m in range(2):
            for part in range(2):
                start = part * HALF + m * NEAR
                out[rows(i * 4 + m * 2 + part, NEAR, WEIGHT), :] = spectrum[
                    start : start + NEAR, i * LANES : (i + 1) * LANES
                ]
    out[rows(8, NEAR, WEIGHT), :] = jnp.broadcast_to(counts, (NEAR, LANES))


def sums_kernel(spread, model, weight, out, power_out):
    leading = place()[3] == NEAR_ORDER[0]
    counts = jnp.sum(weight[rows(8, NEAR, WEIGHT), :], axis=0, keepdims=True)
    residual = jnp.zeros((SHELLS, LANES), jnp.float32)
    for m in range(2):
        packed = jnp.logical_and(leading, m == 0)
        share = jnp.where(packed, 1.0, 2.0) / ANGLES
        left = particle_rows(spread, m)
        sides = []
        for part in range(2):
            sides.append(
                jnp.concatenate(
                    [
                        weight[rows(i * 4 + m * 2 + part, NEAR, WEIGHT), :]
                        for i in range(OWN_PARTICLES)
                    ],
                    axis=0,
                )
            )
        left_t = left.T
        product = dot(left_t, jnp.concatenate(sides, axis=1))
        real_real = product[:SHELLS, :LANES]
        imag_real = product[SHELLS:, :LANES]
        real_imag = product[:SHELLS, LANES:]
        imag_imag = product[SHELLS:, LANES:]
        real = real_real + jnp.where(packed, 0.0, imag_imag)
        imag = jnp.where(packed, imag_imag, imag_real - real_imag)
        energy = jnp.sum(left_t * left_t, axis=1, keepdims=True)
        residual = residual + (energy[:SHELLS] + energy[SHELLS:]) * (share / LANES)
        for part, value in ((0, real), (1, imag)):
            j = 2 * m + part
            ref = model_rows(model, MODEL, j)
            residual = residual + share * ref * (counts * ref - 2.0 * value)
            for far in range(FAR):
                start = FAR_AT[far] * SUMS + j * 8
                out[start : start + 8, :] = value[far * 8 : far * 8 + 8]
    power = dot(jnp.ones((8, LANES), jnp.float32), residual, ((1,), (1,)))
    power = jnp.concatenate([power, jnp.zeros_like(power)], axis=1)
    power_out[...] = jnp.broadcast_to(power[:1], (NEAR, LANES))
    for far in range(FAR):
        start = far * SUMS + 32
        out[start : start + 1, :] = counts


def average_kernel(sums, power, averages, spread_averages):
    total = sums[0:SUMS, :]
    for far in range(1, FAR):
        total = total + sums[far * SUMS : (far + 1) * SUMS, :]
    block = total[:32] / (total[32:33] + 1.0)
    averages[...] = block
    residual = jnp.sum(power[...], axis=0, keepdims=True)
    for far in range(FAR):
        spread_averages[far * NEXT : far * NEXT + 32, :] = block
        spread_averages[far * NEXT + 32 : far * NEXT + 33, :] = residual


def next_kernel(spread, averages, model, out, noise_out):
    leading = place()[3] == NEAR_ORDER[0]
    noise = jnp.sum(model[rows(32, FAR, NEXT), :], axis=0, keepdims=True)[:, :SHELLS]
    noise = noise / (PARTICLES * ANGLES)
    noise_out[...] = noise
    scale = inverse_column(noise)
    half_norm = jnp.zeros((SHELLS, LANES), jnp.float32)
    for m in range(2):
        packed = jnp.logical_and(leading, m == 0)
        share = jnp.where(packed, 0.5, 1.0) / ANGLES
        real = model_rows(model, NEXT, 2 * m)
        imag = model_rows(model, NEXT, 2 * m + 1)
        half_norm = half_norm + share * scale * (real * real + imag * imag)
        cross = cross_rows(particle_rows(spread, m), real * scale, imag * scale, packed)
        store_cross(out, FINAL, m, cross)
    half_norm = jnp.sum(half_norm, axis=0, keepdims=True)
    out[rows(8, NEAR, FINAL), :] = jnp.broadcast_to(half_norm, (NEAR, LANES))
    own = [averages[j * 8 : j * 8 + 8, :] for j in range(4)]
    for c in range(4):
        span = slice(c * OWN_CLASSES, (c + 1) * OWN_CLASSES)
        piece = jnp.concatenate([part[:, span] for part in own], axis=1)
        for side in range(2):
            for shell in range(8):
                start = NEAR_AT[shell * 8 + side * 4 + c] * FINAL + 9
                out[start : start + 1, :] = piece[shell : shell + 1]


def evidence_kernel(final, inverse, averages, evidence):
    quarter, half, _, _ = place()
    half_norm = jnp.sum(final[rows(8, NEAR, FINAL), :], axis=0, keepdims=True)
    lane = lax.broadcasted_iota(jnp.int32, (1, LANES), 1)
    found = jnp.zeros((1, LANES), jnp.float32)
    for i, scores in enumerate(group_scores(final, FINAL, inverse, half_norm)):
        peak = whole(jnp.max, scores)
        total = peak + jnp.log(whole(jnp.sum, jnp.exp(scores - peak)))
        total = total - jnp.log(jnp.full((1, 1), CLASSES * ANGLES, jnp.float32))
        found = found + jnp.where(lane == quarter * OWN_PARTICLES + i, total, 0.0)
    evidence[...] = found[:, :8]
    packed = final[rows(9, NEAR, FINAL), :]
    pieces = []
    for part in range(2):
        for m in range(2):
            j = 2 * m + part
            pieces.append(packed[:, j * OWN_CLASSES : (j + 1) * OWN_CLASSES])
    spectrum = jnp.concatenate(pieces, axis=0)
    table = inverse[pl.ds(pl.multiple_of(half * HALF, HALF), HALF), :]
    averages[...] = dot(table, spectrum).T


VMEM = pl.BlockSpec(memory_space=pltpu.VMEM)
HBM = pl.BlockSpec(memory_space=pltpu.HBM)


def call(kernel, shapes, in_specs, *operands, scratch=(), limit=32 * 1024):
    outs = [jax.ShapeDtypeStruct(shape, jnp.float32) for shape in shapes]
    return pl.pallas_call(
        kernel,
        out_shape=outs,
        in_specs=in_specs,
        out_specs=[VMEM] * len(outs),
        scratch_shapes=scratch,
        compiler_params=pltpu.CompilerParams(vmem_limit_bytes=limit * 1024),
    )(*operands)


def exchange(value, axes, order):
    sent = value.reshape(len(order), 1, value.size // len(order))
    got = lax.all_to_all(sent, axes, 0, 0, tiled=True, axis_index_groups=[order])
    return got.reshape(value.shape)


def shards(particles, references, noise_var):
    forward, inverse = angle_tables()
    noise = noise_var.reshape(1, SHELLS)
    with jax.named_scope("spread"):
        (spread,) = call(
            spread_kernel,
            [(NEAR * SPREAD, LANES)],
            [HBM] * 4,
            noise,
            forward,
            particles,
            references,
            scratch=[
                pltpu.VMEM((1, SHELLS), jnp.float32),
                pltpu.VMEM((ANGLES, ANGLES), jnp.float32),
                pltpu.VMEM((OWN_PARTICLES, SHELLS, ANGLES), jnp.float32),
                pltpu.VMEM((OWN_CLASSES, HALF), jnp.float32),
                pltpu.SemaphoreType.DMA((8,)),
            ],
            limit=60 * 1024,
        )
        spread = exchange(spread, GROUP, NEAR_ORDER)
    with jax.named_scope("model"):
        (model,) = call(model_kernel, [(FAR * MODEL, LANES)], [VMEM], spread)
        model = exchange(model, "far", FAR_ORDER)
    with jax.named_scope("cross"):
        cross, half_norm = call(
            cross_kernel,
            [(NEAR * CROSS, LANES), (8, LANES)],
            [VMEM] * 2,
            spread,
            model,
        )
        cross = exchange(cross, GROUP, NEAR_ORDER)
    with jax.named_scope("posterior"):
        (weight,) = call(
            posterior_kernel,
            [(NEAR * WEIGHT, LANES)],
            [VMEM] * 4,
            cross,
            half_norm,
            forward,
            inverse,
        )
        weight = exchange(weight, GROUP, NEAR_ORDER)
    with jax.named_scope("sums"):
        sums, power = call(
            sums_kernel,
            [(FAR * SUMS, LANES), (NEAR, LANES)],
            [VMEM] * 3,
            spread,
            model,
            weight,
        )
        power = exchange(power, GROUP, NEAR_ORDER)
        sums, power = lax.optimization_barrier((sums, power))
        sums = exchange(sums, "far", FAR_ORDER)
    with jax.named_scope("averages"):
        own, next_model = call(
            average_kernel, [(32, LANES), (FAR * NEXT, LANES)], [VMEM] * 2, sums, power
        )
        next_model = exchange(next_model, "far", FAR_ORDER)
    with jax.named_scope("next"):
        final, noise_new = call(
            next_kernel,
            [(NEAR * FINAL, LANES), (1, SHELLS)],
            [VMEM] * 3,
            spread,
            own,
            next_model,
        )
        final = exchange(final, GROUP, NEAR_ORDER)
    with jax.named_scope("evidence"):
        averages, evidence = call(
            evidence_kernel,
            [(OWN_CLASSES, LANES), (1, 8)],
            [VMEM] * 2,
            final,
            inverse,
        )
        evidence = lax.psum(evidence.reshape(8), "cls")
    return averages, noise_new.reshape(SHELLS), evidence


def solution(mesh):
    split = Mesh(mesh.devices.reshape(FAR, 2, 2, 4, 4), ("far", "near", "h", "x", "cls"))
    dom = ("far", "near", "h", "x")
    return jax.shard_map(
        shards,
        mesh=split,
        in_specs=(P(dom, None, None), P("cls", dom), P()),
        out_specs=(P("cls", dom), P(), P(dom)),
        check_vma=False,
    )
```

```python
import jax
import jax.numpy as jnp
import numpy as np
from jax import lax
from jax.experimental import pallas as pl
from jax.experimental.pallas import tpu as pltpu
from jax.sharding import Mesh, PartitionSpec as P

GROUP = ("near", "h", "x", "cls")
FAR = 8
NEAR = 64
SHELLS = 64
ANGLES = 256
HALF = ANGLES // 2
CLASSES = 128
OWN_CLASSES = 32
OWN_PARTICLES = 2
PARTICLES = 1024
LANES = 128
FAR_ORDER = [3, 1, 7, 6, 5, 2, 0, 4]
NEAR_ORDER = [
    27, 33, 58, 22, 8, 32, 48, 57, 23, 10, 15, 11, 50, 61, 52, 1,
    28, 6, 37, 41, 20, 31, 43, 59, 53, 4, 3, 2, 38, 26, 14, 42,
    63, 17, 45, 44, 60, 47, 55, 12, 16, 5, 35, 25, 21, 19, 34, 24,
    40, 62, 9, 39, 13, 46, 51, 56, 54, 0, 49, 29, 7, 36, 18, 30,
]
FAR_AT = [FAR_ORDER.index(i) for i in range(FAR)]
NEAR_AT = [NEAR_ORDER.index(i) for i in range(NEAR)]


def dot(left, right, contract=((1,), (0,))):
    return lax.dot_general(
        left,
        right,
        (contract, ((), ())),
        precision=lax.Precision.HIGHEST,
        preferred_element_type=jnp.float32,
    )


def angle_tables():
    angle = np.arange(ANGLES)
    slot = np.arange(HALF)
    radians = (slot[:, None] * angle[None, :] % ANGLES) * (2.0 * np.pi / ANGLES)
    sine = -np.sin(radians)
    sine[0] = np.where(angle % 2 == 0, 1.0, -1.0)
    forward = np.concatenate([np.cos(radians), sine], axis=0)
    weight = np.where(slot == 0, 1.0, 2.0) / ANGLES
    inverse = forward * np.concatenate([weight, weight])[:, None]
    return (
        jnp.asarray(forward.astype(np.float32)),
        jnp.asarray(np.ascontiguousarray(inverse.T).astype(np.float32)),
    )


def place():
    near, h, x, cls = (lax.axis_index(name) for name in GROUP)
    shell = lax.axis_index("far") * 8 + near * 4 + h * 2 + lax.shift_right_logical(x, 1)
    return cls, lax.bitwise_and(x, 1), shell, near * 32 + h * 16 + x * 4 + cls


def rows(base, count, stride):
    return pl.ds(base, count, stride=stride)


def halves(image, part):
    return image[:, part * SHELLS : (part + 1) * SHELLS]


SPREAD = 6
MODEL = 33
CROSS = 8
WEIGHT = 9
SUMS = 33
NEXT = 33
FINAL = 10


def inverse_column(noise):
    row = lax.broadcasted_iota(jnp.int32, (SHELLS, SHELLS), 0)
    column = lax.broadcasted_iota(jnp.int32, (SHELLS, SHELLS), 1)
    return 1.0 / jnp.sum(jnp.where(row == column, noise, 0.0), axis=1, keepdims=True)


def spread_kernel(
    noise_ref, table_ref, particles, references, out, noise, forward, images, own_ref, sems
):
    quarter, half, shell, _ = place()
    first = quarter * OWN_PARTICLES
    copies = [
        pltpu.make_async_copy(noise_ref, noise, sems.at[0]),
        pltpu.make_async_copy(references, own_ref, sems.at[1]),
    ]
    for i in range(OWN_PARTICLES):
        copies.append(
            pltpu.make_async_copy(particles.at[first + i], images.at[i], sems.at[2 + i])
        )
    for i in range(4):
        span = pl.ds(i * NEAR, NEAR)
        copies.append(
            pltpu.make_async_copy(table_ref.at[span], forward.at[span], sems.at[4 + i])
        )
    for copy in copies:
        copy.start()
    for copy in copies:
        copy.wait()
    spectrum = dot(
        forward[...], images[...].reshape(OWN_PARTICLES * SHELLS, ANGLES), ((1,), (1,))
    )
    for i in range(OWN_PARTICLES):
        both = jnp.concatenate(
            [halves(spectrum[:HALF], i), halves(spectrum[HALF:], i)], axis=1
        )
        for m in range(2):
            out[rows(i * 2 + m, NEAR, SPREAD), :] = both[m * NEAR : (m + 1) * NEAR]
    own = own_ref[...]
    table = forward[:, pl.ds(pl.multiple_of(half * HALF, HALF), HALF)]
    model = dot(table, own, ((1,), (1,)))
    pieces = []
    for m in range(2):
        for part in range(2):
            start = part * HALF + m * NEAR
            pieces.append(model[start : start + NEAR])
    out[rows(4, NEAR, SPREAD), :] = jnp.concatenate(pieces, axis=1)
    power = dot(jnp.full((8, LANES), 0.5, jnp.float32), own * own, ((1,), (1,)))
    lane = lax.broadcasted_iota(jnp.int32, (1, SHELLS), 1)
    own_noise = jnp.sum(jnp.where(lane == shell, noise[...], 0.0), axis=1, keepdims=True)
    power = jnp.concatenate([power] * 4, axis=1) * (1.0 / own_noise)
    lane = lax.broadcasted_iota(jnp.int32, power.shape, 1)
    power = jnp.where(lane // OWN_CLASSES == quarter, power, 0.0)
    passed = jnp.concatenate([noise[...], jnp.zeros((1, SHELLS), jnp.float32)], axis=1)
    power = power[:1] + jnp.where(quarter == 3, passed, 0.0)
    out[rows(5, NEAR, SPREAD), :] = jnp.broadcast_to(power, (NEAR, LANES))


def model_kernel(spread, out):
    def sent(shell, side, c, row):
        start = NEAR_AT[shell * 8 + side * 4 + c] * SPREAD + row
        return spread[start : start + 1, :]

    by_class = []
    power = jnp.zeros((1, LANES), jnp.float32)
    lane = lax.broadcasted_iota(jnp.int32, (1, LANES), 1)
    for c in range(4):
        models, powers = [], []
        for side in range(2):
            models.append(
                jnp.concatenate([sent(shell, side, c, 4) for shell in range(8)], axis=0)
            )
            powers.append(
                jnp.concatenate([sent(shell, side, c, 5) for shell in range(8)], axis=0)
            )
        by_class.append(models[0] + models[1])
        total = jnp.sum(powers[0] + powers[1], axis=0, keepdims=True)
        power = power + jnp.where(lane // OWN_CLASSES == c, total, 0.0)
    pieces = []
    for j in range(4):
        span = slice(j * OWN_CLASSES, (j + 1) * OWN_CLASSES)
        pieces.append(jnp.concatenate([part[:, span] for part in by_class], axis=1))
    block = jnp.concatenate(pieces, axis=0)
    for far in range(FAR):
        out[far * MODEL : far * MODEL + 32, :] = block
        out[far * MODEL + 32 : far * MODEL + 33, :] = power


def model_rows(model, stride, j):
    return jnp.concatenate(
        [model[at * stride + j * 8 : at * stride + j * 8 + 8, :] for at in FAR_AT],
        axis=0,
    )


def particle_rows(spread, m):
    return jnp.concatenate(
        [spread[rows(i * 2 + m, NEAR, SPREAD), :] for i in range(OWN_PARTICLES)], axis=0
    )


def cross_rows(left, real, imag, packed):
    top = jnp.concatenate([real, jnp.where(packed, 0.0, -imag)], axis=1)
    bottom = jnp.concatenate(
        [jnp.where(packed, 0.0, imag), jnp.where(packed, imag, real)], axis=1
    )
    return dot(left, jnp.concatenate([top, bottom], axis=0))


def store_cross(out, stride, m, cross):
    for i in range(OWN_PARTICLES):
        for part in range(2):
            value = cross[i * NEAR : (i + 1) * NEAR, part * LANES : (part + 1) * LANES]
            out[rows(i * 4 + m * 2 + part, NEAR, stride), :] = value


def cross_kernel(spread, model, out, half_norm):
    leading = place()[3] == NEAR_ORDER[0]
    start = NEAR_AT[3] * SPREAD + 5
    noise = spread[start : start + 1, :]
    scale = inverse_column(noise[:, :SHELLS])
    for m in range(2):
        real = model_rows(model, MODEL, 2 * m) * scale
        imag = model_rows(model, MODEL, 2 * m + 1) * scale
        packed = jnp.logical_and(leading, m == 0)
        store_cross(out, CROSS, m, cross_rows(particle_rows(spread, m), real, imag, packed))
    power = jnp.sum(model[rows(32, FAR, MODEL), :], axis=0, keepdims=True)
    half_norm[...] = jnp.broadcast_to(power, (8, LANES))


def group_scores(cross, stride, inverse, half_norm):
    columns = []
    for i in range(OWN_PARTICLES):
        parts = [
            cross[rows(i * 4 + m * 2 + part, NEAR, stride), :]
            for part in range(2)
            for m in range(2)
        ]
        columns.append(jnp.concatenate(parts, axis=0))
    scores = dot(inverse[...], jnp.concatenate(columns, axis=1))
    return [scores[:, i * LANES : (i + 1) * LANES] - half_norm for i in range(OWN_PARTICLES)]


def whole(reduce, value):
    return reduce(reduce(value, axis=0, keepdims=True), axis=1, keepdims=True)


def posterior_kernel(cross, half_norm, forward, inverse, out):
    posterior = []
    counts = jnp.zeros((1, LANES), jnp.float32)
    for scores in group_scores(cross, CROSS, inverse, half_norm[:1]):
        mass = jnp.exp(scores - whole(jnp.max, scores))
        mass = mass / whole(jnp.sum, mass)
        counts = counts + jnp.sum(mass, axis=0, keepdims=True)
        posterior.append(mass)
    spectrum = dot(forward[...], jnp.concatenate(posterior, axis=1))
    for i in range(OWN_PARTICLES):
        for m in range(2):
            for part in range(2):
                start = part * HALF + m * NEAR
                out[rows(i * 4 + m * 2 + part, NEAR, WEIGHT), :] = spectrum[
                    start : start + NEAR, i * LANES : (i + 1) * LANES
                ]
    out[rows(8, NEAR, WEIGHT), :] = jnp.broadcast_to(counts, (NEAR, LANES))


def sums_kernel(spread, model, weight, out, power_out):
    leading = place()[3] == NEAR_ORDER[0]
    counts = jnp.sum(weight[rows(8, NEAR, WEIGHT), :], axis=0, keepdims=True)
    residual = jnp.zeros((SHELLS, LANES), jnp.float32)
    for m in range(2):
        packed = jnp.logical_and(leading, m == 0)
        share = jnp.where(packed, 1.0, 2.0) / ANGLES
        left = particle_rows(spread, m)
        sides = []
        for part in range(2):
            sides.append(
                jnp.concatenate(
                    [
                        weight[rows(i * 4 + m * 2 + part, NEAR, WEIGHT), :]
                        for i in range(OWN_PARTICLES)
                    ],
                    axis=0,
                )
            )
        left_t = left.T
        product = dot(left_t, jnp.concatenate(sides, axis=1))
        real_real = product[:SHELLS, :LANES]
        imag_real = product[SHELLS:, :LANES]
        real_imag = product[:SHELLS, LANES:]
        imag_imag = product[SHELLS:, LANES:]
        real = real_real + jnp.where(packed, 0.0, imag_imag)
        imag = jnp.where(packed, imag_imag, imag_real - real_imag)
        energy = jnp.sum(left_t * left_t, axis=1, keepdims=True)
        residual = residual + (energy[:SHELLS] + energy[SHELLS:]) * (share / LANES)
        for part, value in ((0, real), (1, imag)):
            j = 2 * m + part
            ref = model_rows(model, MODEL, j)
            residual = residual + share * ref * (counts * ref - 2.0 * value)
            for far in range(FAR):
                start = FAR_AT[far] * SUMS + j * 8
                out[start : start + 8, :] = value[far * 8 : far * 8 + 8]
    power = dot(jnp.ones((8, LANES), jnp.float32), residual, ((1,), (1,)))
    power = jnp.concatenate([power, jnp.zeros_like(power)], axis=1)
    power_out[...] = jnp.broadcast_to(power[:1], (NEAR, LANES))
    for far in range(FAR):
        start = far * SUMS + 32
        out[start : start + 1, :] = counts


def average_kernel(sums, power, averages, spread_averages):
    total = sums[0:SUMS, :]
    for far in range(1, FAR):
        total = total + sums[far * SUMS : (far + 1) * SUMS, :]
    block = total[:32] / (total[32:33] + 1.0)
    averages[...] = block
    residual = jnp.sum(power[...], axis=0, keepdims=True)
    for far in range(FAR):
        spread_averages[far * NEXT : far * NEXT + 32, :] = block
        spread_averages[far * NEXT + 32 : far * NEXT + 33, :] = residual


def next_kernel(spread, averages, model, out, noise_out):
    leading = place()[3] == NEAR_ORDER[0]
    noise = jnp.sum(model[rows(32, FAR, NEXT), :], axis=0, keepdims=True)[:, :SHELLS]
    noise = noise / (PARTICLES * ANGLES)
    noise_out[...] = noise
    scale = inverse_column(noise)
    half_norm = jnp.zeros((SHELLS, LANES), jnp.float32)
    for m in range(2):
        packed = jnp.logical_and(leading, m == 0)
        share = jnp.where(packed, 0.5, 1.0) / ANGLES
        real = model_rows(model, NEXT, 2 * m)
        imag = model_rows(model, NEXT, 2 * m + 1)
        half_norm = half_norm + share * scale * (real * real + imag * imag)
        cross = cross_rows(particle_rows(spread, m), real * scale, imag * scale, packed)
        store_cross(out, FINAL, m, cross)
    half_norm = jnp.sum(half_norm, axis=0, keepdims=True)
    out[rows(8, NEAR, FINAL), :] = jnp.broadcast_to(half_norm, (NEAR, LANES))
    own = [averages[j * 8 : j * 8 + 8, :] for j in range(4)]
    for c in range(4):
        span = slice(c * OWN_CLASSES, (c + 1) * OWN_CLASSES)
        piece = jnp.concatenate([part[:, span] for part in own], axis=1)
        for side in range(2):
            for shell in range(8):
                start = NEAR_AT[shell * 8 + side * 4 + c] * FINAL + 9
                out[start : start + 1, :] = piece[shell : shell + 1]


def evidence_kernel(final, inverse, averages, evidence):
    quarter, half, _, _ = place()
    half_norm = jnp.sum(final[rows(8, NEAR, FINAL), :], axis=0, keepdims=True)
    lane = lax.broadcasted_iota(jnp.int32, (1, LANES), 1)
    found = jnp.zeros((1, LANES), jnp.float32)
    for i, scores in enumerate(group_scores(final, FINAL, inverse, half_norm)):
        peak = whole(jnp.max, scores)
        total = peak + jnp.log(whole(jnp.sum, jnp.exp(scores - peak)))
        total = total - jnp.log(jnp.full((1, 1), CLASSES * ANGLES, jnp.float32))
        found = found + jnp.where(lane == quarter * OWN_PARTICLES + i, total, 0.0)
    evidence[...] = found[:, :8]
    packed = final[rows(9, NEAR, FINAL), :]
    pieces = []
    for part in range(2):
        for m in range(2):
            j = 2 * m + part
            pieces.append(packed[:, j * OWN_CLASSES : (j + 1) * OWN_CLASSES])
    spectrum = jnp.concatenate(pieces, axis=0)
    table = inverse[pl.ds(pl.multiple_of(half * HALF, HALF), HALF), :]
    averages[...] = dot(table, spectrum).T


VMEM = pl.BlockSpec(memory_space=pltpu.VMEM)
HBM = pl.BlockSpec(memory_space=pltpu.HBM)


def call(kernel, shapes, in_specs, *operands, scratch=(), limit=32 * 1024):
    outs = [jax.ShapeDtypeStruct(shape, jnp.float32) for shape in shapes]
    return pl.pallas_call(
        kernel,
        out_shape=outs,
        in_specs=in_specs,
        out_specs=[VMEM] * len(outs),
        scratch_shapes=scratch,
        compiler_params=pltpu.CompilerParams(vmem_limit_bytes=limit * 1024),
    )(*operands)


def exchange(value, axes, order):
    sent = value.reshape(len(order), 1, value.size // len(order))
    got = lax.all_to_all(sent, axes, 0, 0, tiled=True, axis_index_groups=[order])
    return got.reshape(value.shape)


def shards(particles, references, noise_var):
    forward, inverse = angle_tables()
    noise = noise_var.reshape(1, SHELLS)
    with jax.named_scope("spread"):
        (spread,) = call(
            spread_kernel,
            [(NEAR * SPREAD, LANES)],
            [HBM] * 4,
            noise,
            forward,
            particles,
            references,
            scratch=[
                pltpu.VMEM((1, SHELLS), jnp.float32),
                pltpu.VMEM((ANGLES, ANGLES), jnp.float32),
                pltpu.VMEM((OWN_PARTICLES, SHELLS, ANGLES), jnp.float32),
                pltpu.VMEM((OWN_CLASSES, HALF), jnp.float32),
                pltpu.SemaphoreType.DMA((8,)),
            ],
            limit=60 * 1024,
        )
        spread = exchange(spread, GROUP, NEAR_ORDER)
    with jax.named_scope("model"):
        (model,) = call(model_kernel, [(FAR * MODEL, LANES)], [VMEM], spread)
        model = exchange(model, "far", FAR_ORDER)
    with jax.named_scope("cross"):
        cross, half_norm = call(
            cross_kernel,
            [(NEAR * CROSS, LANES), (8, LANES)],
            [VMEM] * 2,
            spread,
            model,
        )
        cross = exchange(cross, GROUP, NEAR_ORDER)
    with jax.named_scope("posterior"):
        (weight,) = call(
            posterior_kernel,
            [(NEAR * WEIGHT, LANES)],
            [VMEM] * 4,
            cross,
            half_norm,
            forward,
            inverse,
        )
        weight = exchange(weight, GROUP, NEAR_ORDER)
    with jax.named_scope("sums"):
        sums, power = call(
            sums_kernel,
            [(FAR * SUMS, LANES), (NEAR, LANES)],
            [VMEM] * 3,
            spread,
            model,
            weight,
        )
        power = exchange(power, GROUP, NEAR_ORDER)
        sums, power = lax.optimization_barrier((sums, power))
        sums = exchange(sums, "far", FAR_ORDER)
    with jax.named_scope("averages"):
        own, next_model = call(
            average_kernel, [(32, LANES), (FAR * NEXT, LANES)], [VMEM] * 2, sums, power
        )
        next_model = exchange(next_model, "far", FAR_ORDER)
    with jax.named_scope("next"):
        final, noise_new = call(
            next_kernel,
            [(NEAR * FINAL, LANES), (1, SHELLS)],
            [VMEM] * 3,
            spread,
            own,
            next_model,
        )
        final = exchange(final, GROUP, NEAR_ORDER)
    with jax.named_scope("evidence"):
        averages, evidence = call(
            evidence_kernel,
            [(OWN_CLASSES, LANES), (1, 8)],
            [VMEM] * 2,
            final,
            inverse,
        )
        evidence = lax.psum(evidence.reshape(8), "cls")
    return averages, noise_new.reshape(SHELLS), evidence


def solution(mesh):
    split = Mesh(mesh.devices.reshape(FAR, 2, 2, 4, 4), ("far", "near", "h", "x", "cls"))
    dom = ("far", "near", "h", "x")
    return jax.shard_map(
        shards,
        mesh=split,
        in_specs=(P(dom, None, None), P("cls", dom), P()),
        out_specs=(P("cls", dom), P(), P(dom)),
        check_vma=False,
    )
```
